32 devices in a mesh: row: 4 (over y, core), col: 8 (over z, x).
Axes of the slice: x: 2, y: 2, z: 4, core: 2. Of those that a mesh axis runs over, the one named last changes fastest.
Arguments:
- tokens: bfloat16 [128, 12288], P('col', 'row'), may hold values from -6 to 6
- norm_gain: float32 [12288], P('row'), may hold values from 0.25 to 90
- norm_bias: float32 [12288], P('row'), may hold values from -3 to 3
- weight_in: bfloat16 [12288, 24576], P('row', 'col'), may hold values from -1 to 1
- weight_out: bfloat16 [24576, 12288], P('col', 'row'), may hold values from -0.0390625 to 0.0390625
- cotangent: bfloat16 [128, 12288], P('col', 'row'), may hold values from -6 to 6
Outputs:
- output: bfloat16 [128, 12288], P('col', 'row')
- input_grad: bfloat16 [128, 12288], P('col', 'row')
- first_grad: bfloat16 [12288, 24576], P('row', 'col')
- second_grad: bfloat16 [24576, 12288], P('col', 'row')
- gain_grad: float32 [12288], P('row')
- bias_grad: float32 [12288], P('row')
The draws below stay inside these ranges and needn't reach their ends.
All inputs are finite; a program needn't handle non-finite values.
Results may differ from the reference program's by a relative error of at most 0.018.
Values may be sent and summed in bfloat16 or wider, within the bound.
A program may use at most 320 MiB of HBM per device.

```python
import jax
import jax.numpy as jnp
from jax import lax

D = 12288
FF = 24576
TOKENS = 128
N_ROW = 4
N_COL = 8


def draw_norm_gain(key, part):
    key = jax.random.fold_in(key, 7)
    noise_key, place_key, level_key = jax.random.split(key, 3)
    position = jnp.arange(D, dtype=jnp.float32) / (D - 1)
    low, high, jitter, top_low, top_high = (0.5, 2.0, 0.2, 40.0, 80.0)
    ramp = low * jnp.exp(jnp.log(high / low) * position)
    noise = jax.random.uniform(noise_key, (D,), jnp.float32, 1.0 - jitter, 1.0 + jitter)
    outlier_count = max(2, D // 1536)
    places = jax.random.randint(place_key, (outlier_count,), 0, D)
    levels = jax.random.uniform(level_key, (outlier_count,), jnp.float32, top_low, top_high)
    matches = jnp.arange(D, dtype=jnp.int32)[:, None] == places[None, :]
    boosted = jnp.max(jnp.where(matches, levels[None, :], 0.0), axis=1)
    gained = jnp.where(jnp.any(matches, axis=1), boosted, ramp * noise)
    return gained.astype(jnp.float32)


def draw_tokens(key, part):
    key = jax.random.fold_in(key, 11)
    noise_key, shift_key = jax.random.split(key)
    position = jnp.arange(D, dtype=jnp.float32) / (D - 1)
    noise = jnp.clip(jax.random.normal(noise_key, (TOKENS, D), jnp.float32), -5.0, 5.0)
    low, high, span = (0.35, 2.0, 0.5)
    profile = low + (high - low) * jnp.sin(jnp.pi * position)
    shift = jax.random.uniform(shift_key, (TOKENS, 1), jnp.float32, -span, span)
    return (noise + shift * profile[None, :]).astype(jnp.bfloat16)


def draw_weight_in(key, part):
    key = jax.random.fold_in(key, 13)
    noise_key, column_key, phase_key = jax.random.split(key, 3)
    position = jnp.arange(D, dtype=jnp.float32) / (D - 1)
    noise = jnp.clip(jax.random.normal(noise_key, (D, FF), jnp.float32), -6.0, 6.0)
    low, high, amplitude, normalizer = (0.3, 3.0, 1.0986123, 0.62)
    ramp = low + (high - low) * position
    column = jnp.clip(jax.random.normal(column_key, (FF,), jnp.float32), -4.0, 4.0)
    extra = 0.08 * ramp[:, None] * column[None, :] * FF ** (-0.5)
    outlier_count = max(2, D // 1536)
    spread = (1.0 + outlier_count * 3600.0 / (1.75 * D)) ** (-0.5)
    phase = jax.random.uniform(phase_key, (), jnp.float32, 0.0, 6.2831853)
    along = jnp.arange(FF, dtype=jnp.float32) / FF
    level = normalizer * spread * jnp.exp(amplitude * jnp.sin(6.2831853 * along + phase))
    return ((noise * D ** (-0.5) + extra) * level[None, :]).astype(jnp.bfloat16)


def level_of(own_key, extent, pieces, least, largest):
    loudness = 1.0
    for dim, parts in pieces:
        draws = jax.random.uniform(jax.random.fold_in(jax.random.fold_in(own_key, 6), dim), (parts,), jnp.float32, least / len(pieces), largest / len(pieces))
        loudness = loudness * jnp.repeat(jnp.exp(draws), extent[dim] // parts).reshape((-1,) + (1,) * (len(extent) - 1 - dim))
    return loudness


def scatter_about(stream_key, extent, scale, limit, cuts=(), held_as=jnp.bfloat16):
    loudness = level_of(stream_key, extent, cuts, -0.22, 0.18) if cuts else 1.0
    array = jax.random.normal(stream_key, extent, jnp.float32) * scale * loudness
    return jnp.minimum(jnp.maximum(array, -limit), limit).astype(held_as)


def setup_inputs(seed: int = 0) -> dict:
    key_list = jax.random.split(jax.random.key(seed), 7)
    tokens = draw_tokens(jax.random.fold_in(key_list[6], 71), 0)
    norm_gain = draw_norm_gain(jax.random.fold_in(key_list[6], 71), 0)
    norm_bias = scatter_about(key_list[2], (D,), 0.5, 3.0, ((0, 4),), jnp.float32)
    weight_in = draw_weight_in(jax.random.fold_in(key_list[6], 71), 0)
    weight_out = scatter_about(key_list[4], (FF, D), FF ** -0.5, 0.0390625, ((0, 8), (1, 4)))
    cotangent = scatter_about(key_list[5], (TOKENS, D), 1.0, 6.0, ((0, 8), (1, 4)))
    return {"tokens": tokens, "norm_gain": norm_gain, "norm_bias": norm_bias, "weight_in": weight_in, "weight_out": weight_out, "cotangent": cotangent}


gelu_scale = 0.7978845608028654
cubic = 0.044715
epsilon = 1e-05

def gelu(value):
    return 0.5 * value * (1.0 + jnp.tanh(gelu_scale * (value + cubic * value * value * value)))

def gelu_slope(value):
    inner = jnp.tanh(gelu_scale * (value + cubic * value * value * value))
    return 0.5 * (1.0 + inner) + 0.5 * value * (1.0 - inner * inner) * gelu_scale * (1.0 + 3.0 * cubic * value * value)

def block_sum(left, right, blocks, right_dim):
    block_width = left.shape[1] // blocks

    def step(carry, index):
        begin = (index * block_width).astype(jnp.int32)
        piece = lax.dynamic_slice_in_dim(left, begin, block_width, 1)
        other = lax.dynamic_slice_in_dim(right, begin, block_width, right_dim)
        term = lax.dot_general(piece, other, (((1,), (right_dim,)), ((), ())), preferred_element_type=jnp.float32)
        rounded = lax.optimization_barrier(term.astype(jnp.bfloat16))
        return (carry + rounded.astype(jnp.float32), None)
    shape = (left.shape[0], right.shape[1 - right_dim])
    result, unused = lax.scan(step, jnp.zeros(shape, jnp.float32), jnp.arange(blocks, dtype=jnp.int32))
    return result

def reference(tokens, norm_gain, norm_bias, weight_in, weight_out, cotangent):
    widened = tokens.astype(jnp.float32)
    mean = lax.optimization_barrier(jnp.sum(widened, axis=1)) / D
    center = widened - mean[:, None]
    variance = lax.optimization_barrier(jnp.sum(center * center, axis=1)) / D
    inverse = lax.rsqrt(variance + epsilon)
    normal = center * inverse[:, None]
    normed = (normal * norm_gain + norm_bias).astype(jnp.bfloat16)
    hidden = block_sum(normed, weight_in, N_ROW, 0)
    activation = gelu(hidden).astype(jnp.bfloat16)
    mixed = block_sum(activation, weight_out, N_COL, 0)
    output = (widened + mixed).astype(jnp.bfloat16)
    grad_act = block_sum(cotangent, weight_out, N_ROW, 1)
    grad_hidden = (grad_act * gelu_slope(hidden)).astype(jnp.bfloat16)
    grad_normed = block_sum(grad_hidden, weight_in, N_COL, 1)
    first = lax.dot_general(normed, grad_hidden, (((0,), (0,)), ((), ())), preferred_element_type=jnp.float32)
    second = lax.dot_general(activation, cotangent, (((0,), (0,)), ((), ())), preferred_element_type=jnp.float32)
    scaled = grad_normed * norm_gain
    sum_one = lax.optimization_barrier(jnp.sum(scaled, axis=1))
    sum_two = lax.optimization_barrier(jnp.sum(scaled * normal, axis=1))
    input_grad = (cotangent.astype(jnp.float32) + inverse[:, None] * (scaled - (sum_one / D)[:, None] - normal * (sum_two / D)[:, None])).astype(jnp.bfloat16)
    gain_part = lax.optimization_barrier(jnp.sum(grad_normed * normal, axis=0))
    bias_part = lax.optimization_barrier(jnp.sum(grad_normed, axis=0))
    squares = jnp.sum(first * first) + jnp.sum(second * second)
    factor = jnp.minimum(1.0, jnp.sqrt(2.0 * D * FF / squares))
    return (output, input_grad, (first * factor).astype(jnp.bfloat16), (second * factor).astype(jnp.bfloat16), gain_part * factor, bias_part * factor)
```

```python
import functools

import jax
import jax.numpy as jnp
from jax import lax
from jax.experimental import pallas as pl
from jax.experimental.pallas import tpu as pltpu
from jax.sharding import PartitionSpec as P

gelu_scale = 0.7978845608028654
cubic = 0.044715
epsilon = 1e-05
CHUNK = 768
MESH = pl.DeviceIdType.MESH
f32, bf16 = jnp.float32, jnp.bfloat16


def chunk_of(width):
    return CHUNK if width % CHUNK == 0 else width


def remote(src, dst, send, recv, dev):
    return pltpu.make_async_remote_copy(
        src_ref=src, dst_ref=dst, send_sem=send, recv_sem=recv, device_id=dev, device_id_type=MESH
    )


class Axis:
    def __init__(self, name, size, total, device):
        self.size, self.half, self.outer = size, total // 2, size // 2
        self.piece = total // size
        self.me = lax.axis_index(name)
        self.o, self.i = self.me // 2, lax.rem(self.me, 2)
        self.device = device

    def out_peer(self, k):
        return lax.rem(self.o + k, self.outer)

    def out_source(self, k):
        return lax.rem(self.o + self.outer - k, self.outer)

    def dev(self, o, i):
        return self.device(o * 2 + i)

    def inner_dev(self):
        return self.dev(self.o, 1 - self.i)

    def rows(self, o, i):
        return pl.ds(pl.multiple_of(i * self.half + o * self.piece, self.piece), self.piece)

    def own(self):
        return self.rows(self.o, self.i)

    def half_rows(self, i):
        return pl.ds(pl.multiple_of(i * self.half, self.half), self.half)

    def in_half(self, o):
        return pl.ds(pl.multiple_of(o * self.piece, self.piece), self.piece)


class Gather:
    def __init__(self, axis, buf, sems):
        self.axis, self.buf = axis, buf
        self.osend, self.orecv, self.isend, self.irecv = sems

    def out_copy(self, n, k, source=False):
        a = self.axis
        o = a.out_source(k) if source else a.o
        ref = self.buf.at[n, a.rows(o, a.i)]
        return remote(ref, ref, self.osend.at[n, k], self.orecv.at[n, k], a.dev(a.out_peer(k), a.i))

    def in_copy(self, n, k, i):
        a = self.axis
        ref = self.buf.at[n, a.rows(a.out_source(k), i)]
        return remote(ref, ref, self.isend.at[n, k], self.irecv.at[n, k], a.inner_dev())

    def begin(self, n):
        for k in range(1, self.axis.outer):
            self.out_copy(n, k).start()
        self.in_copy(n, 0, self.axis.i).start()

    def forward(self, n):
        for k in range(1, self.axis.outer):
            self.out_copy(n, k, True).wait_recv()
            self.in_copy(n, k, self.axis.i).start()

    def finish(self, n):
        for k in range(self.axis.outer):
            self.in_copy(n, k, 1 - self.axis.i).wait_recv()

    def drain(self, n):
        for k in range(self.axis.outer):
            if k:
                self.out_copy(n, k).wait_send()
            self.in_copy(n, k, self.axis.i).wait_send()


class Scatter:
    def __init__(self, axis, part, half, out, sems):
        self.axis, self.part, self.half, self.out = axis, part, half, out
        self.isend, self.irecv, self.osend, self.orecv = sems

    def in_copy(self, n):
        a = self.axis
        return remote(
            self.part.at[n, a.half_rows(1 - a.i)], self.half.at[n],
            self.isend.at[n], self.irecv.at[n], a.inner_dev(),
        )

    def out_copy(self, n, k):
        a = self.axis
        return remote(
            self.half.at[n, a.in_half(a.out_peer(k))], self.out.at[n, k - 1],
            self.osend.at[n, k], self.orecv.at[n, k], a.dev(a.out_peer(k), a.i),
        )

    def begin(self, n, value):
        self.part[n] = value.astype(bf16)
        self.in_copy(n).start()

    def middle(self, n):
        a = self.axis
        self.in_copy(n).wait_recv()
        pair = self.part[n, a.half_rows(a.i), :].astype(f32) + self.half[n].astype(f32)
        self.half[n] = pair.astype(bf16)
        for k in range(1, a.outer):
            self.out_copy(n, k).start()

    def finish(self, n):
        a = self.axis
        total = self.half[n, a.in_half(a.o), :].astype(f32)
        for k in range(1, a.outer):
            self.out_copy(n, k).wait_recv()
            total = total + self.out[n, k - 1].astype(f32)
        return total

    def drain(self, n):
        self.in_copy(n).wait_send()
        for k in range(1, self.axis.outer):
            self.out_copy(n, k).wait_send()


class Direct:
    def __init__(self, axis, size, device, me, place, sems):
        self.size, self.device, self.me, self.place = size, device, me, place
        self.send, self.recv = sems

    def copy(self, k, source=False):
        slot = lax.rem(self.me + self.size - k, self.size) if source else self.me
        ref = self.place(slot)
        peer = self.device(lax.rem(self.me + k, self.size))
        return remote(ref, ref, self.send.at[k], self.recv.at[k], peer)

    def begin(self):
        for k in range(1, self.size):
            self.copy(k).start()

    def finish(self):
        for k in range(1, self.size):
            self.copy(k, True).wait_recv()

    def drain(self):
        for k in range(1, self.size):
            self.copy(k).wait_send()


def contract_last(left, right):
    return lax.dot_general(left, right, (((1,), (1,)), ((), ())), preferred_element_type=f32)


def two(first, second, shape):
    lane = lax.broadcasted_iota(jnp.int32, shape, 1)
    return jnp.where(lane < 64, jnp.broadcast_to(first, shape), jnp.broadcast_to(second, shape))


def exchange_kernel(
    n_row, n_col, nk, nh,
    tokens, gain, bias, win_hbm, wout_hbm, cot_own,
    normed_o, gh_o, act_o, cot_o, factor_o, output_o, igrad_o, gb_o,
    win, wout, tok, cot, normed, act, gh, slope, gn,
    part_h, part_g, part_m, part_n, half_h, half_g, half_m, half_n, out_h, out_g, out_m, out_n,
    rstat, stat, rsum, rsq, csq, gbx, gbz,
    wsem, osem,
    tok_a, tok_b, tok_c, tok_d, cot_a, cot_b, cot_c, cot_d,
    act_a, act_b, act_c, act_d, gh_a, gh_b, gh_c, gh_d,
    h_a, h_b, h_c, h_d, g_a, g_b, g_c, g_d, m_a, m_b, m_c, m_d, n_a, n_b, n_c, n_d,
    rs_a, rs_b, cs_a, cs_b, sum_a, sum_b, rq_a, rq_b, cq_a, cq_b, gx_a, gx_b, gz_a, gz_b,
):
    t0, width = tokens.shape
    total = t0 * n_col
    kc, hc = width // nk, win.shape[1] // nh
    features, hiddens = width * n_row, win.shape[1] * n_col
    my_row, my_col = lax.axis_index("row"), lax.axis_index("col")
    row_dev = lambda r: (r, my_col)
    col_dev = lambda c: (my_row, c)
    row = Axis("row", n_row, total, row_dev)
    col = Axis("col", n_col, total, col_dev)

    loads = []
    for index, (src, dst) in enumerate(((win_hbm, win), (wout_hbm, wout))):
        part = src.shape[0] // 4
        for q in range(4):
            rows = pl.ds(q * part, part)
            loads.append(pltpu.make_async_copy(src.at[rows], dst.at[rows], wsem.at[index * 4 + q]))
    for load in loads:
        load.start()

    barrier = pltpu.get_barrier_semaphore()
    for k in range(1, n_row):
        pl.semaphore_signal(barrier, inc=1, device_id=row_dev(lax.rem(my_row + k, n_row)), device_id_type=MESH)
    for k in range(1, n_col):
        pl.semaphore_signal(barrier, inc=1, device_id=col_dev(lax.rem(my_col + k, n_col)), device_id_type=MESH)

    for n in range(nk):
        tok[n, col.own(), :] = tokens[:, n * kc:(n + 1) * kc]
        cot[n, col.own(), :] = cot_own[:, n * kc:(n + 1) * kc]
    widened = tokens[...].astype(f32)
    local_mean = jnp.sum(widened, axis=1, keepdims=True) / width
    away = widened - local_mean
    rstat[my_row] = two(local_mean, jnp.sum(away * away, axis=1, keepdims=True), (t0, 128))
    pl.semaphore_wait(barrier, n_row + n_col - 2)

    tok_g = Gather(col, tok, (tok_a, tok_b, tok_c, tok_d))
    cot_g = Gather(col, cot, (cot_a, cot_b, cot_c, cot_d))
    act_g = Gather(row, act, (act_a, act_b, act_c, act_d))
    gh_g = Gather(row, gh, (gh_a, gh_b, gh_c, gh_d))
    h_s = Scatter(row, part_h, half_h, out_h, (h_a, h_b, h_c, h_d))
    g_s = Scatter(row, part_g, half_g, out_g, (g_a, g_b, g_c, g_d))
    m_s = Scatter(col, part_m, half_m, out_m, (m_a, m_b, m_c, m_d))
    n_s = Scatter(col, part_n, half_n, out_n, (n_a, n_b, n_c, n_d))
    rstat_d = Direct(row, n_row, row_dev, my_row, lambda s: rstat.at[s], (rs_a, rs_b))
    stat_d = Direct(col, n_col, col_dev, my_col, lambda s: stat.at[col.rows(s // 2, lax.rem(s, 2))], (cs_a, cs_b))
    sum_d = Direct(row, n_row, row_dev, my_row, lambda s: rsum.at[s], (sum_a, sum_b))
    rsq_d = Direct(row, n_row, row_dev, my_row, lambda s: rsq.at[s], (rq_a, rq_b))
    csq_d = Direct(col, n_col, col_dev, my_col, lambda s: csq.at[s], (cq_a, cq_b))
    gb_z = Direct(
        col, n_col // 2, lambda o: col.dev(o, col.i), col.o, lambda s: gbz.at[s], (gz_a, gz_b)
    )
    gb_x = remote(gbx.at[0], gbx.at[1], gx_a, gx_b, col.inner_dev())

    def each(count, body):
        def step(n, carry):
            body(n)
            return carry

        lax.fori_loop(0, count, step, 0)

    def keep(index, src, dst):
        copy = pltpu.make_async_copy(src, dst, osem.at[index])
        copy.start()
        return copy

    rstat_d.begin()
    each(nk, tok_g.begin)
    rstat_d.finish()
    means = [rstat[r][:, 0:1] for r in range(n_row)]
    mean = sum(means) / n_row
    spread = sum(rstat[r][:, 64:65] for r in range(n_row))
    spread = spread + width * sum((m - mean) * (m - mean) for m in means)
    own_inverse = lax.rsqrt(spread / features + epsilon)
    own_mean = mean
    stat[col.own(), :] = two(own_mean, own_inverse, (t0, 128))
    stat_d.begin()
    each(nk, tok_g.forward)
    each(nk, cot_g.begin)
    stat_d.finish()

    def normalize(n):
        tok_g.finish(n)
        normal = (tok[n].astype(f32) - stat[:, 0:1]) * stat[:, 64:65]
        normed[n] = (normal * gain[n] + bias[n]).astype(bf16)

    each(nk, normalize)
    kept = [keep(0, normed, normed_o)]
    for load in loads[:4]:
        load.wait()

    def forward_in(n):
        cols = pl.ds(pl.multiple_of(n * hc, hc), hc)
        h_s.begin(n, sum(
            jnp.dot(normed[k], win[k * kc:(k + 1) * kc, cols], preferred_element_type=f32) for k in range(nk)
        ))

    each(nh, forward_in)
    each(nh, h_s.middle)
    each(nk, cot_g.forward)

    def activate(n):
        v = h_s.finish(n)
        inner = jnp.tanh(gelu_scale * (v + cubic * v * v * v))
        slope[n] = 0.5 * (1.0 + inner) + 0.5 * v * (1.0 - inner * inner) * gelu_scale * (1.0 + 3.0 * cubic * v * v)
        act[n, row.own(), :] = (0.5 * v * (1.0 + inner)).astype(bf16)
        act_g.begin(n)

    each(nh, activate)
    each(nk, cot_g.finish)
    kept.append(keep(1, cot, cot_o))
    for load in loads[4:]:
        load.wait()

    def backward_out(n):
        rows = pl.ds(pl.multiple_of(n * hc, hc), hc)
        g_s.begin(n, sum(contract_last(cot[k], wout[rows, k * kc:(k + 1) * kc]) for k in range(nk)))

    each(nh, backward_out)
    each(nh, act_g.forward)
    each(nh, g_s.middle)
    each(nh, act_g.finish)
    kept.append(keep(2, act, act_o))

    def forward_out(n):
        cols = pl.ds(pl.multiple_of(n * kc, kc), kc)
        m_s.begin(n, sum(
            jnp.dot(act[k], wout[k * hc:(k + 1) * hc, cols], preferred_element_type=f32) for k in range(nh)
        ))

    each(nk, forward_out)

    def slope_times(n):
        gh[n, row.own(), :] = (g_s.finish(n) * slope[n]).astype(bf16)
        gh_g.begin(n)

    each(nh, slope_times)
    each(nk, m_s.middle)
    gram_normed = sum(contract_last(normed[k], normed[k]) for k in range(nk))
    gram_cot = sum(contract_last(cot[k], cot[k]) for k in range(nk))
    gram_act = sum(contract_last(act[k], act[k]) for k in range(nh))
    each(nh, gh_g.forward)
    each(nh, gh_g.finish)
    kept.append(keep(3, gh, gh_o))
    gram_gh = sum(contract_last(gh[k], gh[k]) for k in range(nh))
    products = gram_normed * gram_gh + gram_act * gram_cot
    rsq[my_row] = jnp.broadcast_to(jnp.sum(jnp.sum(products, axis=1, keepdims=True), axis=0, keepdims=True), (8, 128))
    rsq_d.begin()

    if gbx.shape[1] > 2 * nk:
        gbx[0] = jnp.zeros_like(gbx[0])

    def backward_in(n):
        rows = pl.ds(pl.multiple_of(n * kc, kc), kc)
        value = sum(contract_last(gh[k], win[rows, k * hc:(k + 1) * hc]) for k in range(nh))
        n_s.begin(n, value)
        normal = (tok[n].astype(f32) - stat[:, 0:1]) * stat[:, 64:65]
        gbx[0, pl.ds(n, 1), :] = jnp.sum(value * normal, axis=0, keepdims=True)
        gbx[0, pl.ds(nk + n, 1), :] = jnp.sum(value, axis=0, keepdims=True)

    each(nk, backward_in)
    rsq_d.finish()
    csq[my_col] = sum(rsq[r] for r in range(n_row))
    csq_d.begin()
    gb_x.start()
    each(nk, n_s.middle)
    gb_x.wait_recv()
    gbz[col.o] = gbx[0] + gbx[1]
    gb_z.begin()

    for n in range(nk):
        mixed = m_s.finish(n)
        output_o[:, n * kc:(n + 1) * kc] = (tokens[:, n * kc:(n + 1) * kc].astype(f32) + mixed).astype(bf16)

    one = jnp.zeros((t0, 1), f32)
    other = jnp.zeros((t0, 1), f32)
    for n in range(nk):
        grad_normed = n_s.finish(n)
        normal = (tokens[:, n * kc:(n + 1) * kc].astype(f32) - own_mean) * own_inverse
        scaled = grad_normed * gain[n]
        gn[n] = scaled
        one = one + jnp.sum(scaled, axis=1, keepdims=True)
        other = other + jnp.sum(scaled * normal, axis=1, keepdims=True)
    rsum[my_row] = two(one, other, (t0, 128))
    sum_d.begin()

    csq_d.finish()
    squares = jnp.maximum(sum(csq[c] for c in range(n_col)), 0.0)
    factor = jnp.minimum(1.0, jnp.sqrt(2.0 * features * hiddens / squares))
    factor_o[...] = factor
    gb_z.finish()
    gb_o[...] = sum(gbz[o] for o in range(n_col // 2)) * factor[0:1, 0:1]
    sum_d.finish()
    sums = sum(rsum[r] for r in range(n_row))
    for n in range(nk):
        cols = slice(n * kc, (n + 1) * kc)
        normal = (tokens[:, cols].astype(f32) - own_mean) * own_inverse
        igrad_o[:, cols] = (
            cot_own[:, cols].astype(f32)
            + own_inverse * (gn[n] - sums[:, 0:1] / features - normal * (sums[:, 64:65] / features))
        ).astype(bf16)

    for gather, count in ((tok_g, nk), (cot_g, nk), (act_g, nh), (gh_g, nh)):
        each(count, gather.drain)
    for scatter, count in ((h_s, nh), (g_s, nh), (m_s, nk), (n_s, nk)):
        each(count, scatter.drain)
    for direct in (rstat_d, stat_d, sum_d, rsq_d, csq_d, gb_z):
        direct.drain()
    gb_x.wait_send()
    for copy in kept:
        copy.wait()


def gradient_kernel(
    nk, nh, normed, gh, act, cot, factor, output, igrad, gb,
    first_o, second_o, output_o, igrad_o, gain_o, bias_o,
):
    @pl.when(pl.program_id(0) == 0)
    def _():
        output_o[...] = output[...]
        igrad_o[...] = igrad[...]
        gain_o[...] = gb[0:nk, :]
        bias_o[...] = gb[nk:2 * nk, :]

    scale = factor[0:1, 0:1]
    for left, right, out in ((normed, gh, first_o), (act, cot, second_o)):
        flipped = left[0].T
        piece = right.shape[2]
        for j in range(right.shape[0]):
            value = jnp.dot(flipped, right[j], preferred_element_type=f32)
            out[:, j * piece:(j + 1) * piece] = (value * scale).astype(bf16)


def per_device(n_row, n_col, tokens, norm_gain, norm_bias, weight_in, weight_out, cotangent):
    t0, width = tokens.shape
    hidden = weight_in.shape[1]
    total = t0 * n_col
    kc, hc = chunk_of(width), chunk_of(hidden)
    nk, nh = width // kc, hidden // hc
    ro, co = n_row // 2, n_col // 2
    rp, cp = total // n_row, total // n_col
    gb_rows = max(8, 2 * nk)
    gain = norm_gain.reshape(nk, 1, kc)
    bias = norm_bias.reshape(nk, 1, kc)
    vmem = pl.BlockSpec(memory_space=pltpu.VMEM)
    anywhere = pl.BlockSpec(memory_space=pl.ANY)
    V = pltpu.VMEM
    dma = pltpu.SemaphoreType.DMA
    wide, deep = (nk, total, kc), (nh, total, hc)

    def gather_sems(count, outer):
        return [dma((count, outer))] * 4

    def scatter_sems(count, outer):
        return [dma((count,)), dma((count,)), dma((count, outer)), dma((count, outer))]

    scratch = [
        V((width, hidden), bf16), V((hidden, width), bf16),
        V(wide, bf16), V(wide, bf16), V(wide, bf16), V(deep, bf16), V(deep, bf16),
        V((nh, rp, hc), f32), V((nk, cp, kc), f32),
        V(deep, bf16), V(deep, bf16), V(wide, bf16), V(wide, bf16),
        V((nh, total // 2, hc), bf16), V((nh, total // 2, hc), bf16),
        V((nk, total // 2, kc), bf16), V((nk, total // 2, kc), bf16),
        V((nh, max(1, ro - 1), rp, hc), bf16), V((nh, max(1, ro - 1), rp, hc), bf16),
        V((nk, max(1, co - 1), cp, kc), bf16), V((nk, max(1, co - 1), cp, kc), bf16),
        V((n_row, t0, 128), f32), V((total, 128), f32), V((n_row, t0, 128), f32),
        V((n_row, 8, 128), f32), V((n_col, 8, 128), f32),
        V((2, gb_rows, kc), f32), V((co, gb_rows, kc), f32),
        dma((8,)), dma((4,)),
        *gather_sems(nk, co), *gather_sems(nk, co), *gather_sems(nh, ro), *gather_sems(nh, ro),
        *scatter_sems(nh, ro), *scatter_sems(nh, ro), *scatter_sems(nk, co), *scatter_sems(nk, co),
        dma((n_row,)), dma((n_row,)), dma((n_col,)), dma((n_col,)), dma((n_row,)), dma((n_row,)),
        dma((n_row,)), dma((n_row,)), dma((n_col,)), dma((n_col,)), dma, dma, dma((co,)), dma((co,)),
    ]
    S = jax.ShapeDtypeStruct
    mid = pl.pallas_call(
        functools.partial(exchange_kernel, n_row, n_col, nk, nh),
        out_shape=[
            S(wide, bf16), S(deep, bf16), S(deep, bf16), S(wide, bf16), S((8, 128), f32),
            S((t0, width), bf16), S((t0, width), bf16), S((gb_rows, kc), f32),
        ],
        in_specs=[vmem, vmem, vmem, anywhere, anywhere, vmem],
        out_specs=[anywhere] * 4 + [vmem] * 4,
        scratch_shapes=scratch,
        compiler_params=pltpu.CompilerParams(
            collective_id=0, has_side_effects=True, vmem_limit_bytes=60 * 2**20
        ),
    )(tokens, gain, bias, weight_in, weight_out, cotangent)
    tile = 256
    steps = width // tile
    per_k, per_h = kc // tile, hc // tile
    whole = lambda shape: pl.BlockSpec(shape, lambda i: (0,) * len(shape))
    first, second, output, igrad, gain_grad, bias_grad = pl.pallas_call(
        functools.partial(gradient_kernel, nk, nh),
        grid=(steps,),
        out_shape=[
            S((width, hidden), bf16), S((hidden, width), bf16), S((t0, width), bf16), S((t0, width), bf16),
            S((nk, kc), f32), S((nk, kc), f32),
        ],
        in_specs=[
            pl.BlockSpec((1, total, tile), lambda i: (i // per_k, 0, i % per_k)), whole(deep),
            pl.BlockSpec((1, total, tile), lambda i: (i // per_h, 0, i % per_h)), whole(wide),
            whole((8, 128)), whole((t0, width)), whole((t0, width)), whole((gb_rows, kc)),
        ],
        out_specs=[
            pl.BlockSpec((tile, hidden), lambda i: (i, 0)), pl.BlockSpec((hidden // steps, width), lambda i: (i, 0)),
            whole((t0, width)), whole((t0, width)), whole((nk, kc)), whole((nk, kc)),
        ],
        compiler_params=pltpu.CompilerParams(vmem_limit_bytes=40 * 2**20),
    )(*mid)
    return output, igrad, first, second, gain_grad.reshape(width), bias_grad.reshape(width)


def solution(mesh):
    specs = (P("col", "row"), P("row"), P("row"), P("row", "col"), P("col", "row"), P("col", "row"))
    return jax.shard_map(
        functools.partial(per_device, mesh.shape["row"], mesh.shape["col"]),
        mesh=mesh,
        in_specs=specs,
        out_specs=(P("col", "row"), P("col", "row"), P("row", "col"), P("col", "row"), P("row"), P("row")),
        check_vma=False,
    )
```

```python
import functools

import jax
import jax.numpy as jnp
from jax import lax
from jax.experimental import pallas as pl
from jax.experimental.pallas import tpu as pltpu
from jax.sharding import PartitionSpec as P

gelu_scale = 0.7978845608028654
cubic = 0.044715
epsilon = 1e-05
CHUNK = 768
MESH = pl.DeviceIdType.MESH
f32, bf16 = jnp.float32, jnp.bfloat16


def chunk_of(width):
    return CHUNK if width % CHUNK == 0 else width


def remote(src, dst, send, recv, dev):
    return pltpu.make_async_remote_copy(
        src_ref=src, dst_ref=dst, send_sem=send, recv_sem=recv, device_id=dev, device_id_type=MESH
    )


class Axis:
    def __init__(self, name, size, total, device):
        self.size, self.half, self.outer = size, total // 2, size // 2
        self.piece = total // size
        self.me = lax.axis_index(name)
        self.o, self.i = self.me // 2, lax.rem(self.me, 2)
        self.device = device

    def out_peer(self, k):
        return lax.rem(self.o + k, self.outer)

    def out_source(self, k):
        return lax.rem(self.o + self.outer - k, self.outer)

    def dev(self, o, i):
        return self.device(o * 2 + i)

    def inner_dev(self):
        return self.dev(self.o, 1 - self.i)

    def rows(self, o, i):
        return pl.ds(pl.multiple_of(i * self.half + o * self.piece, self.piece), self.piece)

    def own(self):
        return self.rows(self.o, self.i)

    def half_rows(self, i):
        return pl.ds(pl.multiple_of(i * self.half, self.half), self.half)

    def in_half(self, o):
        return pl.ds(pl.multiple_of(o * self.piece, self.piece), self.piece)


class Gather:
    def __init__(self, axis, buf, sems):
        self.axis, self.buf = axis, buf
        self.osend, self.orecv, self.isend, self.irecv = sems

    def out_copy(self, n, k, source=False):
        a = self.axis
        o = a.out_source(k) if source else a.o
        ref = self.buf.at[n, a.rows(o, a.i)]
        return remote(ref, ref, self.osend.at[n, k], self.orecv.at[n, k], a.dev(a.out_peer(k), a.i))

    def in_copy(self, n, k, i):
        a = self.axis
        ref = self.buf.at[n, a.rows(a.out_source(k), i)]
        return remote(ref, ref, self.isend.at[n, k], self.irecv.at[n, k], a.inner_dev())

    def begin(self, n):
        for k in range(1, self.axis.outer):
            self.out_copy(n, k).start()
        self.in_copy(n, 0, self.axis.i).start()

    def forward(self, n):
        for k in range(1, self.axis.outer):
            self.out_copy(n, k, True).wait_recv()
            self.in_copy(n, k, self.axis.i).start()

    def finish(self, n):
        for k in range(self.axis.outer):
            self.in_copy(n, k, 1 - self.axis.i).wait_recv()

    def drain(self, n):
        for k in range(self.axis.outer):
            if k:
                self.out_copy(n, k).wait_send()
            self.in_copy(n, k, self.axis.i).wait_send()


class Scatter:
    def __init__(self, axis, part, half, out, sems):
        self.axis, self.part, self.half, self.out = axis, part, half, out
        self.isend, self.irecv, self.osend, self.orecv = sems

    def in_copy(self, n):
        a = self.axis
        return remote(
            self.part.at[n, a.half_rows(1 - a.i)], self.half.at[n],
            self.isend.at[n], self.irecv.at[n], a.inner_dev(),
        )

    def out_copy(self, n, k):
        a = self.axis
        return remote(
            self.half.at[n, a.in_half(a.out_peer(k))], self.out.at[n, k - 1],
            self.osend.at[n, k], self.orecv.at[n, k], a.dev(a.out_peer(k), a.i),
        )

    def begin(self, n, value):
        self.part[n] = value.astype(bf16)
        self.in_copy(n).start()

    def middle(self, n):
        a = self.axis
        self.in_copy(n).wait_recv()
        pair = self.part[n, a.half_rows(a.i), :].astype(f32) + self.half[n].astype(f32)
        self.half[n] = pair.astype(bf16)
        for k in range(1, a.outer):
            self.out_copy(n, k).start()

    def finish(self, n):
        a = self.axis
        total = self.half[n, a.in_half(a.o), :].astype(f32)
        for k in range(1, a.outer):
            self.out_copy(n, k).wait_recv()
            total = total + self.out[n, k - 1].astype(f32)
        return total

    def drain(self, n):
        self.in_copy(n).wait_send()
        for k in range(1, self.axis.outer):
            self.out_copy(n, k).wait_send()


class Direct:
    def __init__(self, axis, size, device, me, place, sems):
        self.size, self.device, self.me, self.place = size, device, me, place
        self.send, self.recv = sems

    def copy(self, k, source=False):
        slot = lax.rem(self.me + self.size - k, self.size) if source else self.me
        ref = self.place(slot)
        peer = self.device(lax.rem(self.me + k, self.size))
        return remote(ref, ref, self.send.at[k], self.recv.at[k], peer)

    def begin(self):
        for k in range(1, self.size):
            self.copy(k).start()

    def finish(self):
        for k in range(1, self.size):
            self.copy(k, True).wait_recv()

    def drain(self):
        for k in range(1, self.size):
            self.copy(k).wait_send()


def contract_last(left, right):
    return lax.dot_general(left, right, (((1,), (1,)), ((), ())), preferred_element_type=f32)


def two(first, second, shape):
    lane = lax.broadcasted_iota(jnp.int32, shape, 1)
    return jnp.where(lane < 64, jnp.broadcast_to(first, shape), jnp.broadcast_to(second, shape))


def exchange_kernel(
    n_row, n_col, nk, nh,
    tokens, gain, bias, win_hbm, wout_hbm, cot_own,
    normed_o, gh_o, act_o, cot_o, factor_o, output_o, igrad_o, gb_o,
    win, wout, tok, cot, normed, act, gh, slope, gn,
    part_h, part_g, part_m, part_n, half_h, half_g, half_m, half_n, out_h, out_g, out_m, out_n,
    acc, rstat, stat, rsum, rsq, csq, gbx, gbz,
    wsem, osem,
    tok_a, tok_b, tok_c, tok_d, cot_a, cot_b, cot_c, cot_d,
    act_a, act_b, act_c, act_d, gh_a, gh_b, gh_c, gh_d,
    h_a, h_b, h_c, h_d, g_a, g_b, g_c, g_d, m_a, m_b, m_c, m_d, n_a, n_b, n_c, n_d,
    rs_a, rs_b, cs_a, cs_b, sum_a, sum_b, rq_a, rq_b, cq_a, cq_b, gx_a, gx_b, gz_a, gz_b,
):
    t0, width = tokens.shape
    total = t0 * n_col
    kc, hc = width // nk, win.shape[1] // nh
    features, hiddens = width * n_row, win.shape[1] * n_col
    my_row, my_col = lax.axis_index("row"), lax.axis_index("col")
    row_dev = lambda r: (r, my_col)
    col_dev = lambda c: (my_row, c)
    row = Axis("row", n_row, total, row_dev)
    col = Axis("col", n_col, total, col_dev)

    loads = []
    for index, (src, dst) in enumerate(((win_hbm, win), (wout_hbm, wout))):
        pieces = 4 if index else nk
        part = src.shape[0] // pieces
        for q in range(pieces):
            rows = pl.ds(q * part, part)
            loads.append(pltpu.make_async_copy(src.at[rows], dst.at[rows], wsem.at[index * nk + q]))
    for load in loads:
        load.start()

    barrier = pltpu.get_barrier_semaphore()
    for k in range(1, n_row):
        pl.semaphore_signal(barrier, inc=1, device_id=row_dev(lax.rem(my_row + k, n_row)), device_id_type=MESH)
    for k in range(1, n_col):
        pl.semaphore_signal(barrier, inc=1, device_id=col_dev(lax.rem(my_col + k, n_col)), device_id_type=MESH)

    for n in range(nk):
        tok[n, col.own(), :] = tokens[:, n * kc:(n + 1) * kc]
        cot[n, col.own(), :] = cot_own[:, n * kc:(n + 1) * kc]
    widened = tokens[...].astype(f32)
    local_mean = jnp.sum(widened, axis=1, keepdims=True) / width
    away = widened - local_mean
    rstat[my_row] = two(local_mean, jnp.sum(away * away, axis=1, keepdims=True), (t0, 128))
    pl.semaphore_wait(barrier, n_row + n_col - 2)

    tok_g = Gather(col, tok, (tok_a, tok_b, tok_c, tok_d))
    cot_g = Gather(col, cot, (cot_a, cot_b, cot_c, cot_d))
    act_g = Gather(row, act, (act_a, act_b, act_c, act_d))
    gh_g = Gather(row, gh, (gh_a, gh_b, gh_c, gh_d))
    h_s = Scatter(row, part_h, half_h, out_h, (h_a, h_b, h_c, h_d))
    g_s = Scatter(row, part_g, half_g, out_g, (g_a, g_b, g_c, g_d))
    m_s = Scatter(col, part_m, half_m, out_m, (m_a, m_b, m_c, m_d))
    n_s = Scatter(col, part_n, half_n, out_n, (n_a, n_b, n_c, n_d))
    rstat_d = Direct(row, n_row, row_dev, my_row, lambda s: rstat.at[s], (rs_a, rs_b))
    stat_d = Direct(col, n_col, col_dev, my_col, lambda s: stat.at[col.rows(s // 2, lax.rem(s, 2))], (cs_a, cs_b))
    sum_d = Direct(row, n_row, row_dev, my_row, lambda s: rsum.at[s], (sum_a, sum_b))
    rsq_d = Direct(row, n_row, row_dev, my_row, lambda s: rsq.at[s], (rq_a, rq_b))
    csq_d = Direct(col, n_col, col_dev, my_col, lambda s: csq.at[s], (cq_a, cq_b))
    gb_z = Direct(
        col, n_col // 2, lambda o: col.dev(o, col.i), col.o, lambda s: gbz.at[s], (gz_a, gz_b)
    )
    gb_x = remote(gbx.at[0], gbx.at[1], gx_a, gx_b, col.inner_dev())

    def each(count, body):
        def step(n, carry):
            body(n)
            return carry

        lax.fori_loop(0, count, step, 0)

    def stream(count, ready, term, columns, scatter, extra=None):
        if count > 1:
            for n in range(columns):
                acc[n] = jnp.zeros_like(acc[n])

        def step(k):
            ready(k)
            for n in range(columns):
                acc[n] += term(k, n)

        each(count - 1, step)
        ready(count - 1)
        for n in range(columns):
            value = term(count - 1, n)
            if count > 1:
                value = value + acc[n]
            scatter.begin(n, value)
            if extra is not None:
                extra(n, value)

    def chunk(k, size):
        return pl.ds(k * size if isinstance(k, int) else pl.multiple_of(k * size, size), size)

    def ahead(gather, count):
        def ready(k):
            if isinstance(k, int):
                gather.finish(k)
            else:
                gather.forward(k + 1)
                gather.finish(k)

        gather.forward(0)
        return ready

    def keep(index, src, dst):
        copy = pltpu.make_async_copy(src, dst, osem.at[index])
        copy.start()
        return copy

    rstat_d.begin()
    each(nk, tok_g.begin)
    rstat_d.finish()
    means = [rstat[r][:, 0:1] for r in range(n_row)]
    mean = sum(means) / n_row
    spread = sum(rstat[r][:, 64:65] for r in range(n_row))
    spread = spread + width * sum((m - mean) * (m - mean) for m in means)
    own_inverse = lax.rsqrt(spread / features + epsilon)
    own_mean = mean
    stat[col.own(), :] = two(own_mean, own_inverse, (t0, 128))
    stat_d.begin()
    each(nk, tok_g.forward)
    each(nk, cot_g.begin)
    stat_d.finish()

    def normalize(n):
        tok_g.finish(n)
        pltpu.make_async_copy(win_hbm.at[chunk(n, kc)], win.at[chunk(n, kc)], wsem.at[n]).wait()
        normal = (tok[n].astype(f32) - stat[:, 0:1]) * stat[:, 64:65]
        normed[n] = (normal * gain[n] + bias[n]).astype(bf16)

    stream(
        nk, normalize,
        lambda k, n: jnp.dot(normed[k], win[chunk(k, kc), n * hc:(n + 1) * hc], preferred_element_type=f32),
        nh, h_s,
    )
    kept = [keep(0, normed, normed_o)]
    each(nh, h_s.middle)
    each(nk, cot_g.forward)

    def activate(n):
        v = h_s.finish(n)
        inner = jnp.tanh(gelu_scale * (v + cubic * v * v * v))
        slope[n] = 0.5 * (1.0 + inner) + 0.5 * v * (1.0 - inner * inner) * gelu_scale * (1.0 + 3.0 * cubic * v * v)
        act[n, row.own(), :] = (0.5 * v * (1.0 + inner)).astype(bf16)
        act_g.begin(n)

    each(nh, activate)
    for load in loads[nk:]:
        load.wait()
    stream(
        nk, cot_g.finish,
        lambda k, n: contract_last(cot[k], wout[n * hc:(n + 1) * hc, chunk(k, kc)]),
        nh, g_s,
    )
    kept.append(keep(1, cot, cot_o))
    each(nh, act_g.forward)
    each(nh, g_s.middle)
    stream(
        nh, act_g.finish,
        lambda k, n: jnp.dot(act[k], wout[chunk(k, hc), n * kc:(n + 1) * kc], preferred_element_type=f32),
        nk, m_s,
    )
    kept.append(keep(2, act, act_o))

    def slope_times(n):
        gh[n, row.own(), :] = (g_s.finish(n) * slope[n]).astype(bf16)
        gh_g.begin(n)

    each(nh, slope_times)
    gram_normed = sum(contract_last(normed[k], normed[k]) for k in range(nk))
    gram_cot = sum(contract_last(cot[k], cot[k]) for k in range(nk))
    gram_act = sum(contract_last(act[k], act[k]) for k in range(nh))
    if gbx.shape[1] > 2 * nk:
        gbx[0] = jnp.zeros_like(gbx[0])

    def over_tokens(n, value):
        normal = (tok[n].astype(f32) - stat[:, 0:1]) * stat[:, 64:65]
        gbx[0, n:n + 1, :] = jnp.sum(value * normal, axis=0, keepdims=True)
        gbx[0, nk + n:nk + n + 1, :] = jnp.sum(value, axis=0, keepdims=True)

    stream(
        nh, ahead(gh_g, nh),
        lambda k, n: contract_last(gh[k], win[n * kc:(n + 1) * kc, chunk(k, hc)]),
        nk, n_s, over_tokens,
    )
    kept.append(keep(3, gh, gh_o))
    gb_x.start()
    gram_gh = sum(contract_last(gh[k], gh[k]) for k in range(nh))
    products = gram_normed * gram_gh + gram_act * gram_cot
    rsq[my_row] = jnp.broadcast_to(jnp.sum(jnp.sum(products, axis=1, keepdims=True), axis=0, keepdims=True), (8, 128))
    rsq_d.begin()
    each(nk, m_s.middle)
    each(nk, n_s.middle)
    rsq_d.finish()
    csq[my_col] = sum(rsq[r] for r in range(n_row))
    csq_d.begin()
    gb_x.wait_recv()
    gbz[col.o] = gbx[0] + gbx[1]
    gb_z.begin()
    for gather, count in ((tok_g, nk), (cot_g, nk), (act_g, nh), (gh_g, nh)):
        each(count, gather.drain)
    for scatter, count in ((h_s, nh), (g_s, nh)):
        each(count, scatter.drain)

    for n in range(nk):
        mixed = m_s.finish(n)
        output_o[:, n * kc:(n + 1) * kc] = (tokens[:, n * kc:(n + 1) * kc].astype(f32) + mixed).astype(bf16)

    one = jnp.zeros((t0, 1), f32)
    other = jnp.zeros((t0, 1), f32)
    for n in range(nk):
        grad_normed = n_s.finish(n)
        normal = (tokens[:, n * kc:(n + 1) * kc].astype(f32) - own_mean) * own_inverse
        scaled = grad_normed * gain[n]
        gn[n] = scaled
        one = one + jnp.sum(scaled, axis=1, keepdims=True)
        other = other + jnp.sum(scaled * normal, axis=1, keepdims=True)
    rsum[my_row] = two(one, other, (t0, 128))
    sum_d.begin()

    csq_d.finish()
    squares = jnp.maximum(sum(csq[c] for c in range(n_col)), 0.0)
    factor = jnp.minimum(1.0, jnp.sqrt(2.0 * features * hiddens / squares))
    factor_o[...] = factor
    gb_z.finish()
    gb_o[...] = sum(gbz[o] for o in range(n_col // 2)) * factor[0:1, 0:1]
    sum_d.finish()
    sums = sum(rsum[r] for r in range(n_row))
    for n in range(nk):
        cols = slice(n * kc, (n + 1) * kc)
        normal = (tokens[:, cols].astype(f32) - own_mean) * own_inverse
        igrad_o[:, cols] = (
            cot_own[:, cols].astype(f32)
            + own_inverse * (gn[n] - sums[:, 0:1] / features - normal * (sums[:, 64:65] / features))
        ).astype(bf16)

    for scatter in (m_s, n_s):
        each(nk, scatter.drain)
    for direct in (rstat_d, stat_d, sum_d, rsq_d, csq_d, gb_z):
        direct.drain()
    gb_x.wait_send()
    for copy in kept:
        copy.wait()


def gradient_kernel(
    nk, nh, normed, gh, act, cot, factor, output, igrad, gb,
    first_o, second_o, output_o, igrad_o, gain_o, bias_o,
):
    @pl.when(pl.program_id(0) == 0)
    def _():
        output_o[...] = output[...]
        igrad_o[...] = igrad[...]
        kc = gb.shape[1]
        for n in range(nk):
            gain_o[n * kc:(n + 1) * kc] = gb[n, :]
            bias_o[n * kc:(n + 1) * kc] = gb[nk + n, :]

    scale = factor[0:1, 0:1]
    for left, right, out in ((normed, gh, first_o), (act, cot, second_o)):
        flipped = left[0].T
        piece = right.shape[2]
        for j in range(right.shape[0]):
            value = jnp.dot(flipped, right[j], preferred_element_type=f32)
            out[:, j * piece:(j + 1) * piece] = (value * scale).astype(bf16)


def per_device(n_row, n_col, tokens, norm_gain, norm_bias, weight_in, weight_out, cotangent):
    t0, width = tokens.shape
    hidden = weight_in.shape[1]
    total = t0 * n_col
    kc, hc = chunk_of(width), chunk_of(hidden)
    nk, nh = width // kc, hidden // hc
    ro, co = n_row // 2, n_col // 2
    rp, cp = total // n_row, total // n_col
    gb_rows = max(8, 2 * nk)
    gain = norm_gain.reshape(nk, 1, kc)
    bias = norm_bias.reshape(nk, 1, kc)
    vmem = pl.BlockSpec(memory_space=pltpu.VMEM)
    anywhere = pl.BlockSpec(memory_space=pl.ANY)
    V = pltpu.VMEM
    dma = pltpu.SemaphoreType.DMA
    wide, deep = (nk, total, kc), (nh, total, hc)

    def gather_sems(count, outer):
        return [dma((count, outer))] * 4

    def scatter_sems(count, outer):
        return [dma((count,)), dma((count,)), dma((count, outer)), dma((count, outer))]

    scratch = [
        V((width, hidden), bf16), V((hidden, width), bf16),
        V(wide, bf16), V(wide, bf16), V(wide, bf16), V(deep, bf16), V(deep, bf16),
        V((nh, rp, hc), f32), V((nk, cp, kc), f32),
        V(deep, bf16), V(deep, bf16), V(wide, bf16), V(wide, bf16),
        V((nh, total // 2, hc), bf16), V((nh, total // 2, hc), bf16),
        V((nk, total // 2, kc), bf16), V((nk, total // 2, kc), bf16),
        V((nh, max(1, ro - 1), rp, hc), bf16), V((nh, max(1, ro - 1), rp, hc), bf16),
        V((nk, max(1, co - 1), cp, kc), bf16), V((nk, max(1, co - 1), cp, kc), bf16),
        V((max(nk, nh), total, max(kc, hc)), f32),
        V((n_row, t0, 128), f32), V((total, 128), f32), V((n_row, t0, 128), f32),
        V((n_row, 8, 128), f32), V((n_col, 8, 128), f32),
        V((2, gb_rows, kc), f32), V((co, gb_rows, kc), f32),
        dma((nk + 4,)), dma((4,)),
        *gather_sems(nk, co), *gather_sems(nk, co), *gather_sems(nh, ro), *gather_sems(nh, ro),
        *scatter_sems(nh, ro), *scatter_sems(nh, ro), *scatter_sems(nk, co), *scatter_sems(nk, co),
        dma((n_row,)), dma((n_row,)), dma((n_col,)), dma((n_col,)), dma((n_row,)), dma((n_row,)),
        dma((n_row,)), dma((n_row,)), dma((n_col,)), dma((n_col,)), dma, dma, dma((co,)), dma((co,)),
    ]
    S = jax.ShapeDtypeStruct
    mid = pl.pallas_call(
        functools.partial(exchange_kernel, n_row, n_col, nk, nh),
        out_shape=[
            S(wide, bf16), S(deep, bf16), S(deep, bf16), S(wide, bf16), S((8, 128), f32),
            S((t0, width), bf16), S((t0, width), bf16), S((gb_rows, kc), f32),
        ],
        in_specs=[vmem, vmem, vmem, anywhere, anywhere, vmem],
        out_specs=[anywhere] * 4 + [vmem] * 4,
        scratch_shapes=scratch,
        compiler_params=pltpu.CompilerParams(
            collective_id=0, has_side_effects=True, vmem_limit_bytes=60 * 2**20
        ),
    )(tokens, gain, bias, weight_in, weight_out, cotangent)
    tile = 256
    steps = width // tile
    per_k, per_h = kc // tile, hc // tile
    whole = lambda shape: pl.BlockSpec(shape, lambda i: (0,) * len(shape))
    first, second, output, igrad, gain_grad, bias_grad = pl.pallas_call(
        functools.partial(gradient_kernel, nk, nh),
        grid=(steps,),
        out_shape=[
            S((width, hidden), bf16), S((hidden, width), bf16), S((t0, width), bf16), S((t0, width), bf16),
            S((width,), f32), S((width,), f32),
        ],
        in_specs=[
            pl.BlockSpec((1, total, tile), lambda i: (i // per_k, 0, i % per_k)), whole(deep),
            pl.BlockSpec((1, total, tile), lambda i: (i // per_h, 0, i % per_h)), whole(wide),
            whole((8, 128)), whole((t0, width)), whole((t0, width)), whole((gb_rows, kc)),
        ],
        out_specs=[
            pl.BlockSpec((tile, hidden), lambda i: (i, 0)), pl.BlockSpec((hidden // steps, width), lambda i: (i, 0)),
            whole((t0, width)), whole((t0, width)), whole((width,)), whole((width,)),
        ],
        compiler_params=pltpu.CompilerParams(vmem_limit_bytes=60 * 2**20),
    )(*mid)
    return output, igrad, first, second, gain_grad, bias_grad


def solution(mesh):
    specs = (P("col", "row"), P("row"), P("row"), P("row", "col"), P("col", "row"), P("col", "row"))
    return jax.shard_map(
        functools.partial(per_device, mesh.shape["row"], mesh.shape["col"]),
        mesh=mesh,
        in_specs=specs,
        out_specs=(P("col", "row"), P("col", "row"), P("row", "col"), P("col", "row"), P("row"), P("row")),
        check_vma=False,
    )
```
